128 devices in a mesh: lists: 8 (over x, core), score: 16 (over y, z).
Axes of the slice: x: 4, y: 4, z: 4, core: 2. Of those that a mesh axis runs over, the one named last changes fastest.
Arguments:
- queries: bfloat16 [512, 32, 128], P('score', 'lists'), may hold values from -0.59765625 to 0.59765625
- centroids: bfloat16 [65536, 128], P('lists'), may hold values from -3 to 3
- codes: bfloat16 [4096, 128, 128], P(('lists', 'score')), may hold values from -6 to 6
- scales: float32 [4096, 128], P(('lists', 'score')), may hold values from 0.1 to 1
- centroid_ids: int32 [4096, 128], P(('lists', 'score')), may hold values from 0 to 8191
- lengths: int32 [4096], P(('lists', 'score')), may hold values from 1 to 128
- owners: int32 [8, 512, 8], P('lists', 'score'), may hold values from 0 to 127, all different within a row; in each aligned block of 32 rows (0 to 31, 32 to 63, ..., all dimensions but the last counted through in order) at most 4 rows name the same one
- slots: int32 [8, 512, 8], P('lists', 'score'), may hold values from 0 to 31
Outputs:
- scores: float32 [8, 512, 8], P('lists', 'score')
- relevance: float32 [512, 65536], P('score', 'lists')
The draws below stay inside these ranges and needn't reach their ends.
Inputs may be any that keep to these rules, and one draw needn't show every extreme that they name: Within the 32 rows of one device (aligned blocks of 32 rows, the first two dimensions taken together in order) no owner is named more than 4 times; each row names 8 different owners. Owner d holds blocks d * 32 to d * 32 + 31. `centroid_ids`: A row among the 8192 centroids of the block's lists shard.
All inputs are finite; a program needn't handle non-finite values.
Results may differ from the reference program's by a relative error of at most 0.00034.
Values may be sent and summed in bfloat16 or wider, within the bound.
No kernel may reach another device: no remote copies, remote signals or barrier semaphores. Data moves between devices by JAX's collectives and lax.ppermute only.
A program may use at most 128 MiB of HBM per device.

```python
import math
import jax
import jax.numpy as jnp
import numpy as np
from jax import lax

DIM = 128
QT = 32
PT = 128
CENT_DEV = 8192
Q_DEV = 32
CSL = 8
BLK_DEV = 32
NCENT = 65536
Q = 512
BLOCKS = 4096
SHARD_BLOCKS = 512
CAP = 4
N_LISTS = 8
DEVICES = 128


def place_ends(array, key, low, largest):
    index_at = [jax.random.randint(jax.random.fold_in(key, axis), (), 0, length) for axis, length in enumerate(array.shape)]
    main_axis = array.shape.index(max(array.shape))
    beside = index_at[:main_axis] + [(index_at[main_axis] + 1) % array.shape[main_axis]] + index_at[main_axis + 1:]
    return array.at[tuple(index_at)].set(low).at[tuple(beside)].set(largest)


def block_scale(rng, extent, pieces, least, largest):
    def one(dim, parts):
        steps = jax.random.uniform(jax.random.fold_in(jax.random.fold_in(rng, 6), dim), (parts,), jnp.float32, least / len(pieces), largest / len(pieces))
        return jnp.repeat(jnp.exp(steps), extent[dim] // parts).reshape((-1,) + (1,) * (len(extent) - dim - 1))

    loudness = one(*pieces[0])
    for cut in pieces[1:]:
        loudness = loudness * one(*cut)
    return loudness


def routed_block(rng, own, number, rows, count, top, limit, slope):
    order = jax.random.permutation(rng, count)
    packed, usual = portions_of(count, rows * top, limit, slope, True), portions_of(count, rows * top, limit, slope, False)
    places = jnp.arange(count)

    def named(sizes, offset_by):
        used = int((sizes > 0).sum())
        fixed = max(1, used // 4)
        moved = fixed + (places - fixed + offset_by * (used - fixed)) % max(1, count - fixed)
        return jnp.zeros((count,), jnp.int32).at[order[jnp.where(places < fixed, places, moved)]].set(jnp.asarray(sizes, jnp.int32))

    sizes = jnp.where(number % 4 == 0, named(packed, number // 4), named(usual, number - number // 4 - 1))
    mixed = jax.random.permutation(jax.random.fold_in(own, 3), count)
    giver, receiver = mixed[0:count // 2 * 2:2], mixed[1:count // 2 * 2:2]
    margin = jnp.minimum(sizes[giver] - 1, limit - sizes[receiver]) // 2
    margin = jnp.where((giver == order[0]) | (receiver == order[0]) | (sizes[receiver] == 0), 0, jnp.maximum(margin, 0))
    moved = jax.random.randint(jax.random.fold_in(own, 4), (count // 2,), 0, 1 << 20) % (margin + 1)
    sizes = sizes.at[giver].add(-moved).at[receiver].add(moved)
    items = jnp.searchsorted(jnp.cumsum(sizes), jnp.arange(rows * top), side="right").astype(jnp.int32)
    table = items.reshape(top, rows).T
    table = table[jax.random.permutation(jax.random.fold_in(own, 1), rows)]
    offset_by = jax.random.randint(jax.random.fold_in(own, 2), (rows, 1), 0, top)
    return jnp.take_along_axis(table, (jnp.arange(top)[None, :] + offset_by) % top, axis=1)


def portions_of(count, total, limit, lean, full):
    loads = [(1 << 20) // math.isqrt(standing ** lean) + 1 for standing in range(1, count + 1)]
    largest = limit if full else min(limit, max(-(-total // count), total * loads[0] // sum(loads)))
    least = 1 if total - largest >= count - 1 else 0
    given, rest = [largest] + [least] * (count - 1), total - largest - least * (count - 1)
    while rest > 0:
        free = [i for i in range(1, count) if given[i] < largest] or [i for i in range(1, count) if given[i] < limit]
        whole, left = sum([loads[i] for i in free]), rest
        for i in free:
            extra = min(limit - given[i], max(1, left * loads[i] // whole), rest)
            given[i] = given[i] + extra
            rest = rest - extra
    return np.array(given)


def centred(rng, shape, deviation, bound, pieces=(), kind=jnp.bfloat16):
    gain = block_scale(rng, shape, pieces, -0.22, 0.18) if pieces else 1.0
    result = jax.random.normal(rng, shape, jnp.float32) * deviation * gain
    return jnp.minimum(jnp.maximum(result, -bound), bound).astype(kind)


def setup_inputs(seed: int = 0) -> dict:
    key_list = jax.random.split(jax.random.key(seed), 9)
    queries = centred(key_list[0], (Q, QT, DIM), 0.1, 0.59765625, ((0, 16), (1, 8)))
    centroids = centred(key_list[1], (NCENT, DIM), 0.5, 3.0, ((0, 8),))
    codes = centred(key_list[2], (BLOCKS, PT, DIM), 1.0, 6.0, ((0, 128),))
    scales = jnp.clip(jnp.exp(math.log(1.0) - 2.3025851 * jax.random.uniform(key_list[3], (BLOCKS, PT), jnp.float32) ** block_scale(key_list[3], (BLOCKS, PT), ((0, 128),), -0.2, 0.2)), 0.1, 1.0)
    centroid_ids = place_ends(jax.random.randint(key_list[4], (BLOCKS, PT), 0, CENT_DEV), jax.random.fold_in(key_list[4], 1), 0, CENT_DEV - 1).astype(jnp.int32)
    lengths = place_ends(jax.random.randint(key_list[5], (BLOCKS,), 1, PT + 1), jax.random.fold_in(key_list[5], 1), 1, PT).astype(jnp.int32)
    owners_keys = jax.random.split(jax.random.fold_in(key_list[6], 1), N_LISTS * Q // Q_DEV)
    owners_turns = jax.random.permutation(jax.random.fold_in(key_list[6], 3), N_LISTS * Q // Q_DEV)
    owners = jax.vmap(lambda own, number: routed_block(jax.random.fold_in(key_list[6], 2), own, number, Q_DEV, DEVICES, CSL, CAP, 2))(owners_keys, owners_turns).reshape((N_LISTS, Q, CSL))
    slots = place_ends(jax.random.randint(key_list[7], (N_LISTS, Q, CSL), 0, BLK_DEV), jax.random.fold_in(key_list[7], 1), 0, BLK_DEV - 1).astype(jnp.int32)
    return dict(queries=queries, centroids=centroids, codes=codes, scales=scales, centroid_ids=centroid_ids, lengths=lengths, owners=owners, slots=slots)


def rebuild(codes, scales, centroid_ids, centroids, wanted):
    shard = wanted // SHARD_BLOCKS
    rows_index = shard[..., None] * CENT_DEV + centroid_ids[wanted]
    base = centroids[rows_index].astype(jnp.float32)
    vectors = base + scales[wanted][..., None] * codes[wanted].astype(jnp.float32)
    return vectors.astype(jnp.bfloat16)


def reference(queries, centroids, codes, scales, centroid_ids, lengths, owners, slots):
    query_float = queries.astype(jnp.float32)
    block = (owners * BLK_DEV + slots).astype(jnp.int32)

    def score_shard(block_shard):
        vectors = rebuild(codes, scales, centroid_ids, centroids, block_shard)
        inner = jnp.einsum("qtd,qcpd->qctp", query_float, vectors.astype(jnp.float32))
        spots = jnp.arange(PT, dtype=jnp.int32)
        keep = spots[None, None, None, :] < lengths[block_shard][:, :, None, None]
        best = jnp.max(jnp.where(keep, inner, -1e30), axis=3)
        return jnp.sum(best, axis=2) / QT

    scores = lax.map(score_shard, block)
    group = math.gcd(NCENT, 4096)
    flat = queries.reshape(Q * QT, DIM)
    grouped = centroids.reshape(NCENT // group, group, DIM)

    def relate(block_rows):
        inner = lax.dot_general(flat, block_rows, (((1,), (1,)), ((), ())), preferred_element_type=jnp.float32)
        return jnp.max(inner.reshape(Q, QT, group), axis=1)

    related = lax.map(relate, grouped)
    relevance = jnp.transpose(related, (1, 0, 2)).reshape(Q, NCENT)
    return scores, relevance
```

```python
import jax
import jax.numpy as jnp
from jax import lax
from jax.experimental import pallas as pl
from jax.experimental.pallas import tpu as pltpu
from jax.sharding import PartitionSpec as P

AXES = ("lists", "score")
SIDE = 4
CORES = 2
DEVICES = 128
CAP = 4
SMEM = pltpu.SMEM
VMEM = pltpu.VMEM


def device_of(x, core, y, z):
    x, y, z = x % SIDE, y % SIDE, z % SIDE
    return ((x * CORES + core) * SIDE + y) * SIDE + z


def moved(value, step):
    pairs = []
    for x in range(SIDE):
        for core in range(CORES):
            for y in range(SIDE):
                for z in range(SIDE):
                    pairs.append((device_of(x, core, y, z), device_of(*step(x, core, y, z))))
    return lax.ppermute(value, AXES, pairs)


def along_x(k):
    return lambda x, core, y, z: (x + k, core, y, z)


def along_first(k):
    return lambda x, core, y, z: (x, core, y + k, z) if core == 0 else (x, core, y, z + k)


def along_second(k):
    return lambda x, core, y, z: (x, core, y, z + k) if core == 0 else (x, core, y + k, z)


def other_core(x, core, y, z):
    return (x, 1 - core, y, z)


def rebuild_kernel(ids_ref, cent_ref, scale_ref, code_ref, out_ref, table, base):
    b = pl.program_id(0)

    @pl.when(b == 0)
    def _():
        table[...] = cent_ref[...].astype(jnp.float32)

    rows = base.shape[0]
    for p in range(rows):
        base[pl.ds(p, 1), :] = table[pl.ds(ids_ref[b, p], 1), :]
    scale = jnp.transpose(jnp.broadcast_to(scale_ref[0], (rows, rows)))
    out_ref[0] = (base[...] + scale * code_ref[0].astype(jnp.float32)).astype(jnp.bfloat16)


def rebuild(codes, scales, centroid_ids, centroids):
    held, rows, width = codes.shape
    return pl.pallas_call(
        rebuild_kernel,
        grid=(held,),
        out_shape=jax.ShapeDtypeStruct(codes.shape, jnp.bfloat16),
        in_specs=[
            pl.BlockSpec(memory_space=SMEM),
            pl.BlockSpec(centroids.shape, lambda b: (0, 0)),
            pl.BlockSpec((1, 1, rows), lambda b: (b, 0, 0)),
            pl.BlockSpec((1, rows, width), lambda b: (b, 0, 0)),
        ],
        out_specs=pl.BlockSpec((1, rows, width), lambda b: (b, 0, 0)),
        scratch_shapes=[
            VMEM(centroids.shape, jnp.float32),
            VMEM((rows, width), jnp.float32),
        ],
        compiler_params=pltpu.CompilerParams(vmem_limit_bytes=32 << 20),
        cost_estimate=pl.CostEstimate(flops=12000000, bytes_accessed=20000000, transcendentals=0),
        name="rebuild",
    )(centroid_ids, centroids, scales.reshape(held, 1, rows), codes)


UNROLL = 8


def maxsim_kernel(
    where_ref, lengths_ref, own_ref, other_ref, held_ref, out_ref, meta, table, rows_ref, work, sem
):
    groups = SIDE * SIDE
    per = own_ref.shape[0] // groups
    queries = per - 1
    sources = groups * SIDE
    me, my_x, my_core, my_y, my_z = (where_ref[i] for i in range(5))
    for half, ref in enumerate((own_ref, other_ref)):
        for i in range(groups):
            meta[pl.ds((half * groups + i) * 16, 16), :] = ref[i * per + queries].astype(jnp.float32)
    count = 2 * sources
    lane = lax.broadcasted_iota(jnp.int32, (count, 128), 1)
    parts = [meta[pl.ds(row, count, stride=4), :] for row in range(4)]
    hit, slot = jnp.zeros((count, 128), jnp.float32), jnp.zeros((count, 128), jnp.float32)
    for owner, place in ((parts[0], parts[2]), (parts[1], parts[3])):
        mine = owner == me.astype(jnp.float32)
        hit += jnp.where(mine, 1.0, 0.0)
        slot += jnp.where(mine, place, 0.0)
    for shift in (64, 32):
        hit = hit + pltpu.roll(hit, shift, 1)
        slot = slot + pltpu.roll(slot, shift, 1)
    row_id = lax.broadcasted_iota(jnp.int32, (128, 128), 0)
    lane_id = lax.broadcasted_iota(jnp.int32, (128, 128), 1)
    earlier = jnp.where((row_id < queries) & (row_id < lane_id), 1.0, 0.0).astype(jnp.bfloat16)
    prior = jnp.dot(hit.astype(jnp.bfloat16), earlier, preferred_element_type=jnp.float32)
    inside = jnp.where(lane < queries, hit, 0.0)
    code = lane.astype(jnp.float32) * 32.0 + slot
    packed = jnp.where(lane == CAP, jnp.sum(inside, axis=1, keepdims=True), 0.0)
    for rank in range(CAP):
        chosen = jnp.where((inside > 0.5) & (prior == float(rank)), code, 0.0)
        packed = packed + jnp.where(lane == rank, jnp.sum(chosen, axis=1, keepdims=True), 0.0)
    flat = jnp.transpose(packed)[:8].astype(jnp.int32)
    u = lax.broadcasted_iota(jnp.int32, (8, 128), 1)
    line = lax.broadcasted_iota(jnp.int32, (8, 128), 0)
    half = u >> 6
    at = (u >> 2) & 15
    kx = u & 3
    first, second = at & 3, at >> 2
    turned = first * 4 + second
    own_at = jnp.where(half == 0, at, turned)
    other_at = jnp.where(half == 0, turned, at)
    core = my_core ^ half
    dy = jnp.where(core == 0, first, second)
    dz = jnp.where(core == 0, second, first)
    source = (((((my_x - kx) & 3) * 2 + core) * 4) + ((my_y - dy) & 3)) * 4 + ((my_z - dz) & 3)
    table[...] = jnp.where(
        line == 5,
        own_at * per,
        jnp.where(line == 6, other_at * per, jnp.where(line == 7, source * CAP, flat)),
    )
    copy = pltpu.make_async_copy(table, rows_ref, sem)
    copy.start()
    copy.wait()

    def gather_list(step, start):
        for i in range(4):
            src = step * 4 + i
            for rank in range(CAP):
                work[start + rank] = rows_ref[rank, src] + (src << 10) + (rank << 17)
            start = start + rows_ref[CAP, src]
        return start

    total = lax.fori_loop(0, 2 * sources // 4, gather_list, 0)
    for i in range(UNROLL):
        work[total + i] = CAP << 17
    spots = lax.broadcasted_iota(jnp.int32, (32, 128), 1)
    buffer = out_ref

    def one(n):
        item = work[n]
        place = item & 31
        query = (item >> 5) & 31
        src = (item >> 10) & 127
        rank = item >> 17
        token = jnp.concatenate(
            [own_ref[rows_ref[5, src] + query], other_ref[rows_ref[6, src] + query]], axis=0
        )
        inner = lax.dot_general(
            token, held_ref[place], (((1,), (1,)), ((), ())), preferred_element_type=jnp.float32
        )
        kept = jnp.where(spots < lengths_ref[place], inner, -1e30)
        best = jnp.max(kept, axis=1, keepdims=True)
        value = jnp.sum(best, axis=0, keepdims=True) * (1.0 / 32.0)
        dest = jnp.where(rank == CAP, DEVICES * CAP, rows_ref[7, src] + rank)
        return dest, value

    def steps(step, carry):
        done = [one(step * UNROLL + i) for i in range(UNROLL)]
        for dest, value in done:
            buffer[pl.ds(dest, 1), :] = jnp.broadcast_to(value, (1, 128))
        return carry

    lax.fori_loop(0, (total + UNROLL - 1) // UNROLL, steps, 0)


def maxsim(where, lengths, own, other, held):
    rows = DEVICES * CAP + 8
    return pl.pallas_call(
        maxsim_kernel,
        out_shape=jax.ShapeDtypeStruct((rows, 128), jnp.float32),
        in_specs=[pl.BlockSpec(memory_space=SMEM)] * 2 + [pl.BlockSpec(memory_space=VMEM)] * 3,
        out_specs=pl.BlockSpec(memory_space=VMEM),
        scratch_shapes=[
            VMEM((DEVICES * 4, 128), jnp.float32),
            VMEM((8, 128), jnp.int32),
            SMEM((8, 128), jnp.int32),
            SMEM((DEVICES * CAP + 16,), jnp.int32),
            pltpu.SemaphoreType.DMA,
        ],
        compiler_params=pltpu.CompilerParams(vmem_limit_bytes=32 << 20),
        cost_estimate=pl.CostEstimate(flops=12000000, bytes_accessed=20000000, transcendentals=0),
        name="maxsim",
    )(where, lengths, own, other, held)


def final_kernel(owner_ref, back_ref, out_ref):
    queries, per = owner_ref.shape
    lane = lax.broadcasted_iota(jnp.int32, (queries, 128), 1)
    named = [lane == owner_ref[:, c : c + 1] for c in range(per)]
    match = jnp.zeros((queries, 128), jnp.float32)
    for mine in named:
        match += jnp.where(mine, 1.0, 0.0)
    row = lax.broadcasted_iota(jnp.int32, (queries, queries), 0)
    col = lax.broadcasted_iota(jnp.int32, (queries, queries), 1)
    prior = jnp.dot(
        jnp.where(col < row, 1.0, 0.0).astype(jnp.bfloat16),
        match.astype(jnp.bfloat16),
        preferred_element_type=jnp.float32,
    )
    back = jnp.transpose(back_ref[...])
    chosen = jnp.zeros((queries, 128), jnp.float32)
    for rank in range(CAP):
        chosen = jnp.where(prior == float(rank), back[rank : rank + 1, :], chosen)
    spot = lax.broadcasted_iota(jnp.int32, (queries, per), 1)
    out = jnp.zeros((queries, per), jnp.float32)
    for c in range(per):
        value = jnp.sum(jnp.where(named[c], chosen, 0.0), axis=1, keepdims=True)
        out = jnp.where(spot == c, value, out)
    out_ref[...] = out


def final(owners, back):
    return pl.pallas_call(
        final_kernel,
        out_shape=jax.ShapeDtypeStruct(owners.shape, jnp.float32),
        in_specs=[pl.BlockSpec(memory_space=VMEM)] * 2,
        out_specs=pl.BlockSpec(memory_space=VMEM),
        name="final",
    )(owners, back)


def relevance_of(tokens, centroids):
    token_count, query_rows, width = tokens.shape
    inner = lax.dot_general(
        tokens.reshape(token_count * query_rows, width),
        centroids,
        (((1,), (1,)), ((), ())),
        preferred_element_type=jnp.float32,
    )
    return jnp.max(inner.reshape(token_count, query_rows, -1), axis=0)


def per_device(queries, centroids, codes, scales, centroid_ids, lengths, owners, slots):
    query_rows = queries.shape[0]
    owner, slot = owners[0], slots[0]
    meta = jnp.concatenate([owner.T.reshape(2, 128), slot.T.reshape(2, 128)], axis=0)
    first = jnp.concatenate([queries, meta.astype(jnp.bfloat16)[None]], axis=0)
    by_x = jnp.stack([first] + [moved(first, along_x(k)) for k in range(1, SIDE)], axis=1)
    by_x = by_x.reshape(query_rows + 1, SIDE * 4, 128)
    second = jnp.stack([by_x] + [moved(by_x, along_first(k)) for k in range(1, SIDE)], axis=0)
    pieces = [second] + [moved(second, along_second(k)) for k in range(1, SIDE)]
    peers = [moved(piece, other_core) for piece in pieces]
    own = jnp.concatenate(pieces, axis=0).reshape(-1, SIDE * 4, 128)
    other = jnp.concatenate(peers, axis=0).reshape(-1, SIDE * 4, 128)

    lists, score = lax.axis_index("lists"), lax.axis_index("score")
    where = jnp.stack(
        [lists * 16 + score, lists // 2, lists % 2, score // SIDE, score % SIDE]
    ).astype(jnp.int32)
    held = rebuild(codes, scales, centroid_ids, centroids)
    totals = maxsim(where, lengths, own, other, held)
    outgoing = totals[: DEVICES * CAP, 0].reshape(DEVICES, 1, CAP)
    back = lax.all_to_all(outgoing, AXES, split_axis=0, concat_axis=0, tiled=True)
    back = jnp.pad(back.reshape(DEVICES, CAP), ((0, 0), (0, 128 - CAP)))
    scores = final(owner, back)
    tokens = jnp.concatenate([by_x[:query_rows], peers[0][0, :query_rows]], axis=1)
    relevance = relevance_of(jnp.swapaxes(tokens, 0, 1), centroids)
    return (scores[None], relevance)


def solution(mesh):
    placed = (
        P("score", "lists", None),
        P("lists", None),
        P(("lists", "score"), None, None),
        P(("lists", "score"), None),
        P(("lists", "score"), None),
        P(("lists", "score")),
        P("lists", "score", None),
        P("lists", "score", None),
    )
    return jax.shard_map(
        per_device,
        mesh=mesh,
        in_specs=placed,
        out_specs=(P("lists", "score", None), P("score", "lists")),
        check_vma=False,
    )
```

```python
import jax
import jax.numpy as jnp
from jax import lax
from jax.experimental import pallas as pl
from jax.experimental.pallas import tpu as pltpu
from jax.sharding import PartitionSpec as P

AXES = ("lists", "score")
SIDE = 4
CORES = 2
DEVICES = 128
CAP = 4
SMEM = pltpu.SMEM
VMEM = pltpu.VMEM


def device_of(x, core, y, z):
    x, y, z = x % SIDE, y % SIDE, z % SIDE
    return ((x * CORES + core) * SIDE + y) * SIDE + z


def moved(value, step):
    pairs = []
    for x in range(SIDE):
        for core in range(CORES):
            for y in range(SIDE):
                for z in range(SIDE):
                    pairs.append((device_of(x, core, y, z), device_of(*step(x, core, y, z))))
    return lax.ppermute(value, AXES, pairs)


def along_x(k):
    return lambda x, core, y, z: (x + k, core, y, z)


def along_first(k):
    return lambda x, core, y, z: (x, core, y + k, z) if core == 0 else (x, core, y, z + k)


def along_second(k):
    return lambda x, core, y, z: (x, core, y, z + k) if core == 0 else (x, core, y + k, z)


def other_core(x, core, y, z):
    return (x, 1 - core, y, z)


def rebuild_kernel(ids_ref, cent_ref, scale_ref, code_ref, _, out_ref, table, base):
    step = pl.program_id(0)

    @pl.when(step == 0)
    def _():
        table[...] = cent_ref[...].astype(jnp.float32)

    blocks, rows = code_ref.shape[:2]

    def one(b, carry):
        for p in range(rows):
            base[pl.ds(p, 1), :] = table[pl.ds(ids_ref[step * blocks + b, p], 1), :]
        scale = jnp.transpose(jnp.broadcast_to(scale_ref[b], (rows, rows)))
        value = base[...] + scale * code_ref[b].astype(jnp.float32)
        out_ref[b] = value.astype(jnp.bfloat16)
        return carry

    lax.fori_loop(0, blocks, one, 0)


def rebuild(codes, scales, centroid_ids, centroids, after):
    held, rows, width = codes.shape
    step = held // REBUILD_STEPS
    return pl.pallas_call(
        rebuild_kernel,
        grid=(REBUILD_STEPS,),
        out_shape=jax.ShapeDtypeStruct(codes.shape, jnp.bfloat16),
        in_specs=[
            pl.BlockSpec(memory_space=SMEM),
            pl.BlockSpec(centroids.shape, lambda b: (0, 0)),
            pl.BlockSpec((step, 1, rows), lambda b: (b, 0, 0)),
            pl.BlockSpec((step, rows, width), lambda b: (b, 0, 0)),
            pl.BlockSpec(memory_space=pl.ANY),
        ],
        out_specs=pl.BlockSpec((step, rows, width), lambda b: (b, 0, 0)),
        scratch_shapes=[
            VMEM(centroids.shape, jnp.float32),
            VMEM((rows, width), jnp.float32),
        ],
        compiler_params=pltpu.CompilerParams(vmem_limit_bytes=56 << 20),
        cost_estimate=pl.CostEstimate(flops=12000000, bytes_accessed=20000000, transcendentals=0),
        name="rebuild",
    )(centroid_ids, centroids, scales.reshape(held, 1, rows), codes, after)


REBUILD_STEPS = 4
CHUNK = 8
TOGETHER = 8
PLACES = 768
DUMMY_ROW = DEVICES * CAP
ALL = [(k, j, 4 * k + j) for k in range(SIDE) for j in range(SIDE)]
EARLY = [(k, j, 4 * n + j) for n, k in enumerate((0, 1, 3)) for j in (0, 1, 3)]
LATE = [(2, j, j) for j in range(4)] + [(k, 2, 4 + n) for n, k in enumerate((0, 1, 3))]


def as_bf16(mask):
    return jnp.where(mask, 1.0, 0.0).astype(jnp.bfloat16)


def product(a, b):
    return jnp.dot(a.astype(jnp.bfloat16), b, preferred_element_type=jnp.float32)


def by_row(row, values):
    result = jnp.full(row.shape, values[-1], jnp.int32)
    for i, value in enumerate(values[:-1]):
        result = jnp.where(row == i, value, result)
    return result


def request_list(rows, where_ref, own_ref, other_ref, meta):
    per = PER
    queries = per - 1
    me, my_x, my_core, my_y, my_z = (where_ref[i] for i in range(5))
    if len(rows) < 16:
        meta[...] = jnp.full(meta.shape, -1.0, jnp.float32)
    for half, ref in enumerate((own_ref, other_ref)):
        for i, (_, _, at) in enumerate(rows):
            meta[pl.ds((half * 16 + i) * 16, 16), :] = ref[at * per + queries].astype(jnp.float32)
    square = (DEVICES, 128)
    lane = lax.broadcasted_iota(jnp.int32, square, 1)
    line = lax.broadcasted_iota(jnp.int32, square, 0)
    lane_low, lane_high = lane & 31, lane >> 5
    line_low, line_high = line & 31, line >> 5
    same_low = as_bf16(line_low == lane_low)
    same_high = as_bf16(line_high == lane_high)
    parts = [meta[pl.ds(row, DEVICES, stride=4), :] for row in range(4)]
    mine = [parts[i] == me.astype(jnp.float32) for i in range(2)]
    hit = jnp.where(mine[0], 1.0, 0.0) + jnp.where(mine[1], 1.0, 0.0)
    slot = jnp.where(mine[0], parts[2], 0.0) + jnp.where(mine[1], parts[3], 0.0)
    earlier = as_bf16(line_low < lane_low)
    prior = product(hit, earlier)
    hit, slot = product(hit, same_low), product(slot, same_low)
    chosen = (hit > 0.5) & (prior == lane_high.astype(jnp.float32))
    low = lane_low.astype(jnp.float32)
    asked_query = product(jnp.where(chosen, low + 1.0, 0.0), same_high)
    asked_slot = product(jnp.where(chosen, slot, 0.0), same_high)
    wants = (asked_query > 0.5) & (asked_slot == low)
    before = product(jnp.where(lane < line, 1.0, 0.0), as_bf16(wants))
    count = jnp.sum(jnp.where(wants, 1.0, 0.0), axis=0, keepdims=True)
    count = jnp.broadcast_to(count, (8, 128))
    lower_ranks = product(count, as_bf16((line_low == lane_low) & (line_high < lane_high)))
    in_block = product(count, same_low)
    chunks = ((in_block.astype(jnp.int32) + (CHUNK - 1)) // CHUNK).astype(jnp.float32)
    first_chunk = product(chunks, as_bf16((line < 32) & (line < lane_low)))
    all_chunks = product(chunks, as_bf16(line < 32)).astype(jnp.int32)
    spot = before + lower_ranks[:1]
    spot_high = (spot.astype(jnp.int32) // CHUNK).astype(jnp.float32)
    spot_low = spot - spot_high * float(CHUNK)
    high = product(jnp.where(wants, spot_high + first_chunk[:1], 0.0), same_high)
    low_part = product(jnp.where(wants, spot_low, 0.0), same_high)
    spot = jnp.where(asked_query > 0.5, high * float(CHUNK) + low_part, -1.0).astype(jnp.int32)
    fields = [line.astype(jnp.float32), asked_query, asked_slot]
    u_row = lax.broadcasted_iota(jnp.int32, (8, 128), 1).astype(jnp.float32)
    kind = lax.broadcasted_iota(jnp.int32, (8, 128), 0)
    asked = [jnp.transpose(value) for value in fields[1:]]
    to = lax.broadcasted_iota(jnp.int32, (DEVICES, PLACES), 1)
    found = jnp.zeros((8, PLACES), jnp.float32)
    for rank in range(CAP):
        at = 32 * rank
        left = jnp.where(
            kind == 0,
            u_row,
            jnp.where(
                kind == 1,
                asked[0][at : at + 1, :],
                jnp.where(kind == 2, asked[1][at : at + 1, :], float(rank)),
            ),
        )
        found = found + product(left, as_bf16(spot[:, at : at + 1] == to))
    found = found.astype(jnp.int32)
    u, query, slot, rank = (found[i : i + 1, :] for i in range(4))
    half = u >> 6
    at = (u >> 2) & 15
    kx = u & 3
    if len(rows) == 16:
        straight, turned = at, (at & 3) * 4 + (at >> 2)
        first, second = at & 3, at >> 2
    else:
        places = {(k, j): i for k, j, i in rows}
        straight = by_row(at, [i for _, _, i in rows])
        turned = by_row(at, [places[j, k] for k, j, _ in rows])
        first, second = by_row(at, [j for _, j, _ in rows]), by_row(at, [k for k, _, _ in rows])
    own_at = jnp.where(half == 0, straight, turned) * per + query - 1
    other_at = jnp.where(half == 0, turned, straight) * per + query - 1
    core = my_core ^ half
    dy = jnp.where(core == 0, first, second)
    dz = jnp.where(core == 0, second, first)
    source = (((((my_x - kx) & 3) * 2 + core) * 4) + ((my_y - dy) & 3)) * 4 + ((my_z - dz) & 3)
    real = query > 0
    item = jnp.where(real, slot + (own_at << 5) + (other_at << 15), 0)
    goal = jnp.where(real, source + rank * DEVICES, DUMMY_ROW)
    return item, goal, all_chunks[:1]


PER = 33


def maxsim_kernel(
    rows, last, where_ref, lengths_ref, own_ref, other_ref, held_ref, best_in, out_ref, meta, table, work, best, sem
):
    if best is None:
        best = out_ref
    elif best_in is not None:
        best[...] = best_in[...]
    item, goal, all_chunks = request_list(rows, where_ref, own_ref, other_ref, meta)
    table[0:1, :] = item
    table[1:2, :] = goal
    table[2:3, 0:128] = all_chunks
    copy = pltpu.make_async_copy(table, work, sem)
    copy.start()
    copy.wait()
    total = work[2, 0]
    slots_id = lax.broadcasted_iota(jnp.int32, (128, CHUNK * 32), 0)
    group = lax.broadcasted_iota(jnp.int32, (1, 128), 1) >> 5

    def one(chunk):
        tokens = []
        for i in range(CHUNK):
            item = work[0, chunk * CHUNK + i]
            if i == 0:
                block = item & 31
            tokens.append(own_ref[(item >> 5) & 1023])
            tokens.append(other_ref[item >> 15])
        inner = lax.dot_general(
            held_ref[block],
            jnp.concatenate(tokens, axis=0),
            (((1,), (1,)), ((), ())),
            preferred_element_type=jnp.float32,
        )
        kept = jnp.where(slots_id < lengths_ref[block], inner, -1e30)
        return jnp.max(kept, axis=0, keepdims=True)

    def steps(step, carry):
        done = [one(step * TOGETHER + i) for i in range(TOGETHER)]
        for i, value in enumerate(done):
            for j in range(CHUNK):
                part = value[:, j // 4 * 128 : j // 4 * 128 + 128]
                dest = work[1, (step * TOGETHER + i) * CHUNK + j]
                best[pl.ds(dest, 1), :] = jnp.where(group == j % 4, part, 0.0)
        return carry

    lax.fori_loop(0, (total + TOGETHER - 1) // TOGETHER, steps, 0)
    if last:
        lane = lax.broadcasted_iota(jnp.int32, (DEVICES, 128), 1)
        result = jnp.zeros((DEVICES, 128), jnp.float32)
        for rank in range(CAP):
            value = jnp.sum(best[pl.ds(rank * DEVICES, DEVICES), :], axis=1, keepdims=True)
            result = jnp.where(lane == rank, value * (1.0 / 32.0), result)
        out_ref[...] = result


def maxsim(where, lengths, own, other, held, rows=ALL, last=True, best=None):
    def body(*refs):
        refs = list(refs)
        if best is None:
            refs.insert(5, None)
        if not last:
            refs.insert(-1, None)
        maxsim_kernel(rows, last, *refs)

    buffer = (DEVICES * CAP + 8, 128)
    scratch = [
        VMEM((DEVICES * 4, 128), jnp.float32),
        VMEM((8, PLACES), jnp.int32),
        SMEM((8, PLACES), jnp.int32),
    ]
    if last:
        scratch.append(VMEM(buffer, jnp.float32))
    operands = (where, lengths, own, other, held) + (() if best is None else (best,))
    return pl.pallas_call(
        body,
        out_shape=jax.ShapeDtypeStruct((DEVICES, 128) if last else buffer, jnp.float32),
        in_specs=[pl.BlockSpec(memory_space=SMEM)] * 2
        + [pl.BlockSpec(memory_space=VMEM)] * (len(operands) - 2),
        out_specs=pl.BlockSpec(memory_space=VMEM),
        scratch_shapes=scratch + [pltpu.SemaphoreType.DMA],
        compiler_params=pltpu.CompilerParams(vmem_limit_bytes=32 << 20),
        cost_estimate=pl.CostEstimate(flops=12000000, bytes_accessed=20000000, transcendentals=0),
        name="maxsim_late" if last else "maxsim_early",
    )(*operands)


def pack_kernel(query_ref, owner_ref, slot_ref, out_ref):
    queries = query_ref.shape[0]
    out_ref[:queries] = query_ref[...]
    lane = lax.broadcasted_iota(jnp.int32, (1, 128), 1) >> 5
    rows = []
    for ref in (owner_ref, slot_ref):
        wide = ref[...].astype(jnp.float32)
        wide = jnp.concatenate([wide] * 4, axis=1)
        for part in range(2):
            row = jnp.zeros((1, 128), jnp.float32)
            for i in range(4):
                c = part * 4 + i
                row = jnp.where(lane == i, wide[c : c + 1, :], row)
            rows.append(row)
    out_ref[queries] = jnp.concatenate(rows, axis=0).astype(jnp.bfloat16)


def pack(queries, owners, slots):
    rows, tokens, width = queries.shape
    return pl.pallas_call(
        pack_kernel,
        out_shape=jax.ShapeDtypeStruct((rows + 1, tokens, width), jnp.bfloat16),
        in_specs=[pl.BlockSpec(memory_space=VMEM)] * 3,
        out_specs=pl.BlockSpec(memory_space=VMEM),
        name="pack",
    )(queries, owners, slots)


def final_kernel(owner_ref, back_ref, out_ref):
    per, queries = owner_ref.shape
    lane = lax.broadcasted_iota(jnp.int32, (128, queries), 0)
    named = [lane == owner_ref[c : c + 1, :] for c in range(per)]
    match = jnp.zeros((128, queries), jnp.float32)
    for mine in named:
        match += jnp.where(mine, 1.0, 0.0)
    row = lax.broadcasted_iota(jnp.int32, (queries, queries), 0)
    col = lax.broadcasted_iota(jnp.int32, (queries, queries), 1)
    prior = jnp.dot(
        match.astype(jnp.bfloat16), as_bf16(row < col), preferred_element_type=jnp.float32
    )
    back = back_ref[...]
    chosen = jnp.zeros((128, queries), jnp.float32)
    for rank in range(CAP):
        chosen = jnp.where(prior == float(rank), back[:, rank : rank + 1], chosen)
    for c in range(per):
        out_ref[c : c + 1, :] = jnp.sum(jnp.where(named[c], chosen, 0.0), axis=0, keepdims=True)


def final(owners, back):
    return pl.pallas_call(
        final_kernel,
        out_shape=jax.ShapeDtypeStruct(owners.shape, jnp.float32),
        in_specs=[pl.BlockSpec(memory_space=VMEM)] * 2,
        out_specs=pl.BlockSpec(memory_space=VMEM),
        name="final",
    )(owners, back)


def relevance_of(tokens, centroids):
    token_count, query_rows, width = tokens.shape
    inner = lax.dot_general(
        tokens.reshape(token_count * query_rows, width),
        centroids,
        (((1,), (1,)), ((), ())),
        preferred_element_type=jnp.float32,
    )
    return jnp.max(inner.reshape(token_count, query_rows, -1), axis=0)


def per_device(queries, centroids, codes, scales, centroid_ids, lengths, owners, slots):
    query_rows = queries.shape[0]
    owner, slot = owners[0].T, slots[0].T
    first = pack(queries, owner, slot)
    by_x = jnp.stack([first] + [moved(first, along_x(k)) for k in range(1, SIDE)], axis=1)
    by_x = by_x.reshape(query_rows + 1, SIDE * 4, 128)
    second = jnp.stack([by_x] + [moved(by_x, along_first(k)) for k in range(1, SIDE)], axis=0)
    pieces = [second] + [moved(second, along_second(k)) for k in range(1, SIDE)]
    peers = [moved(piece, other_core) for piece in pieces]
    own = jnp.concatenate(pieces, axis=0).reshape(-1, SIDE * 4, 128)
    other = jnp.concatenate(peers, axis=0).reshape(-1, SIDE * 4, 128)

    lists, score = lax.axis_index("lists"), lax.axis_index("score")
    where = jnp.stack(
        [lists * 16 + score, lists // 2, lists % 2, score // SIDE, score % SIDE]
    ).astype(jnp.int32)
    held = rebuild(codes, scales, centroid_ids, centroids, second)
    totals = maxsim(where, lengths, own, other, held)
    outgoing = totals.reshape(DEVICES, 1, 128)
    back = lax.all_to_all(outgoing, AXES, split_axis=0, concat_axis=0, tiled=True)
    scores = final(owner, back.reshape(DEVICES, 128)).T
    tokens = jnp.concatenate([by_x[:query_rows], peers[0][0, :query_rows]], axis=1)
    relevance = relevance_of(jnp.swapaxes(tokens, 0, 1), centroids)
    return (scores[None], relevance)


def solution(mesh):
    placed = (
        P("score", "lists", None),
        P("lists", None),
        P(("lists", "score"), None, None),
        P(("lists", "score"), None),
        P(("lists", "score"), None),
        P(("lists", "score")),
        P("lists", "score", None),
        P("lists", "score", None),
    )
    return jax.shard_map(
        per_device,
        mesh=mesh,
        in_specs=placed,
        out_specs=(P("lists", "score", None), P("score", "lists")),
        check_vma=False,
    )
```

```python
import jax
import jax.numpy as jnp
from jax import lax
from jax.experimental import pallas as pl
from jax.experimental.pallas import tpu as pltpu
from jax.sharding import PartitionSpec as P

AXES = ("lists", "score")
SIDE = 4
CORES = 2
DEVICES = 128
CAP = 4
SMEM = pltpu.SMEM
VMEM = pltpu.VMEM


def device_of(x, core, y, z):
    x, y, z = x % SIDE, y % SIDE, z % SIDE
    return ((x * CORES + core) * SIDE + y) * SIDE + z


def moved(value, step):
    pairs = []
    for x in range(SIDE):
        for core in range(CORES):
            for y in range(SIDE):
                for z in range(SIDE):
                    pairs.append((device_of(x, core, y, z), device_of(*step(x, core, y, z))))
    return lax.ppermute(value, AXES, pairs)


def along_x(k):
    return lambda x, core, y, z: (x + k, core, y, z)


def along_first(k):
    return lambda x, core, y, z: (x, core, y + k, z) if core == 0 else (x, core, y, z + k)


def along_second(k):
    return lambda x, core, y, z: (x, core, y, z + k) if core == 0 else (x, core, y + k, z)


def other_core(x, core, y, z):
    return (x, 1 - core, y, z)


def rebuild_kernel(ids_ref, cent_ref, scale_ref, code_ref, _, out_ref, table, base):
    step = pl.program_id(0)

    @pl.when(step == 0)
    def _():
        table[...] = cent_ref[...].astype(jnp.float32)

    blocks, rows = code_ref.shape[:2]

    def one(b, carry):
        for p in range(rows):
            base[pl.ds(p, 1), :] = table[pl.ds(ids_ref[step * blocks + b, p], 1), :]
        scale = jnp.transpose(jnp.broadcast_to(scale_ref[b], (rows, rows)))
        value = base[...] + scale * code_ref[b].astype(jnp.float32)
        out_ref[b] = value.astype(jnp.bfloat16)
        return carry

    lax.fori_loop(0, blocks, one, 0)


def rebuild(codes, scales, centroid_ids, centroids, after):
    held, rows, width = codes.shape
    step = held // REBUILD_STEPS
    return pl.pallas_call(
        rebuild_kernel,
        grid=(REBUILD_STEPS,),
        out_shape=jax.ShapeDtypeStruct(codes.shape, jnp.bfloat16),
        in_specs=[
            pl.BlockSpec(memory_space=SMEM),
            pl.BlockSpec(centroids.shape, lambda b: (0, 0)),
            pl.BlockSpec((step, 1, rows), lambda b: (b, 0, 0)),
            pl.BlockSpec((step, rows, width), lambda b: (b, 0, 0)),
            pl.BlockSpec(memory_space=pl.ANY),
        ],
        out_specs=pl.BlockSpec((step, rows, width), lambda b: (b, 0, 0)),
        scratch_shapes=[
            VMEM(centroids.shape, jnp.float32),
            VMEM((rows, width), jnp.float32),
        ],
        compiler_params=pltpu.CompilerParams(vmem_limit_bytes=56 << 20),
        cost_estimate=pl.CostEstimate(flops=12000000, bytes_accessed=20000000, transcendentals=0),
        name="rebuild",
    )(centroid_ids, centroids, scales.reshape(held, 1, rows), codes, after)


REBUILD_STEPS = 4
CHUNK = 8
TOGETHER = 16
PLACES = 768
DUMMY_ROW = DEVICES * CAP
X_STEPS = (0, 1, 2, 3)
FIRST_STEPS = (0, 1, 2, 3)
SECOND_STEPS = (0, 1, 3, 2)


def as_bf16(mask):
    return jnp.where(mask, 1.0, 0.0).astype(jnp.bfloat16)


def product(a, b):
    return jnp.dot(a.astype(jnp.bfloat16), b, preferred_element_type=jnp.float32)


def picked(place, values):
    result = jnp.full(place.shape, values[-1], jnp.int32)
    for i, value in enumerate(values[:-1]):
        result = jnp.where(place == i, value, result)
    return result


def request_list(where_ref, own_ref, other_ref, meta):
    per = PER
    queries = per - 1
    me, my_x, my_core, my_y, my_z = (where_ref[i] for i in range(5))
    for half, ref in enumerate((own_ref, other_ref)):
        for i in range(SIDE * SIDE):
            meta[pl.ds((half * 16 + i) * 16, 16), :] = ref[i * per + queries].astype(jnp.float32)
    square = (DEVICES, 128)
    lane = lax.broadcasted_iota(jnp.int32, square, 1)
    line = lax.broadcasted_iota(jnp.int32, square, 0)
    lane_low, lane_high = lane & 31, lane >> 5
    line_low, line_high = line & 31, line >> 5
    same_low = as_bf16(line_low == lane_low)
    same_high = as_bf16(line_high == lane_high)
    parts = [meta[pl.ds(row, DEVICES, stride=4), :] for row in range(4)]
    mine = [parts[i] == me.astype(jnp.float32) for i in range(2)]
    hit = jnp.where(mine[0], 1.0, 0.0) + jnp.where(mine[1], 1.0, 0.0)
    slot = jnp.where(mine[0], parts[2], 0.0) + jnp.where(mine[1], parts[3], 0.0)
    earlier = as_bf16(line_low < lane_low)
    prior = product(hit, earlier)
    hit, slot = product(hit, same_low), product(slot, same_low)
    chosen = (hit > 0.5) & (prior == lane_high.astype(jnp.float32))
    low = lane_low.astype(jnp.float32)
    asked_query = product(jnp.where(chosen, low + 1.0, 0.0), same_high)
    asked_slot = product(jnp.where(chosen, slot, 0.0), same_high)
    wants = (asked_query > 0.5) & (asked_slot == low)
    before = product(jnp.where(lane < line, 1.0, 0.0), as_bf16(wants))
    count = jnp.sum(jnp.where(wants, 1.0, 0.0), axis=0, keepdims=True)
    count = jnp.broadcast_to(count, (8, 128))
    lower_ranks = product(count, as_bf16((line_low == lane_low) & (line_high < lane_high)))
    in_block = product(count, same_low)
    chunks = ((in_block.astype(jnp.int32) + (CHUNK - 1)) // CHUNK).astype(jnp.float32)
    first_chunk = product(chunks, as_bf16((line < 32) & (line < lane_low)))
    all_chunks = product(chunks, as_bf16(line < 32)).astype(jnp.int32)
    spot = before + lower_ranks[:1]
    spot_high = (spot.astype(jnp.int32) // CHUNK).astype(jnp.float32)
    spot_low = spot - spot_high * float(CHUNK)
    high = product(jnp.where(wants, spot_high + first_chunk[:1], 0.0), same_high)
    low_part = product(jnp.where(wants, spot_low, 0.0), same_high)
    spot = jnp.where(asked_query > 0.5, high * float(CHUNK) + low_part, -1.0).astype(jnp.int32)
    fields = [line.astype(jnp.float32), asked_query, asked_slot]
    u_row = lax.broadcasted_iota(jnp.int32, (8, 128), 1).astype(jnp.float32)
    kind = lax.broadcasted_iota(jnp.int32, (8, 128), 0)
    asked = [jnp.transpose(value) for value in fields[1:]]
    to = lax.broadcasted_iota(jnp.int32, (DEVICES, PLACES), 1)
    found = jnp.zeros((8, PLACES), jnp.float32)
    for rank in range(CAP):
        at = 32 * rank
        left = jnp.where(
            kind == 0,
            u_row,
            jnp.where(
                kind == 1,
                asked[0][at : at + 1, :],
                jnp.where(kind == 2, asked[1][at : at + 1, :], float(rank)),
            ),
        )
        found = found + product(left, as_bf16(spot[:, at : at + 1] == to))
    found = found.astype(jnp.int32)
    u, query, slot, rank = (found[i : i + 1, :] for i in range(4))
    half = u >> 6
    at = (u >> 2) & 15
    kx = picked(u & 3, X_STEPS)
    first, second = picked(at & 3, FIRST_STEPS), picked(at >> 2, SECOND_STEPS)
    turned_second = picked(at & 3, [SECOND_STEPS.index(step) for step in FIRST_STEPS])
    turned_first = picked(at >> 2, [FIRST_STEPS.index(step) for step in SECOND_STEPS])
    straight, turned = at, turned_second * 4 + turned_first
    own_at = jnp.where(half == 0, straight, turned) * per + query - 1
    other_at = jnp.where(half == 0, turned, straight) * per + query - 1
    core = my_core ^ half
    dy = jnp.where(core == 0, first, second)
    dz = jnp.where(core == 0, second, first)
    source = (((((my_x - kx) & 3) * 2 + core) * 4) + ((my_y - dy) & 3)) * 4 + ((my_z - dz) & 3)
    real = query > 0
    item = jnp.where(real, slot + (own_at << 5) + (other_at << 15), 0)
    goal = jnp.where(real, source + rank * DEVICES, DUMMY_ROW)
    return item, goal, all_chunks[:1]


PER = 33


def maxsim_kernel(
    where_ref, lengths_ref, own_ref, other_ref, held_ref, out_ref, meta, table, work, best, sem
):
    item, goal, all_chunks = request_list(where_ref, own_ref, other_ref, meta)
    for i in range(PLACES // 128):
        table[i : i + 1, :] = item[:, i * 128 : i * 128 + 128]
        table[8 + i : 9 + i, :] = goal[:, i * 128 : i * 128 + 128]
    table[7:8, :] = all_chunks
    copy = pltpu.make_async_copy(table, work, sem)
    copy.start()
    copy.wait()
    total = work[7, 0]
    slots_id = lax.broadcasted_iota(jnp.int32, (128, CHUNK * 32), 0)
    group = lax.broadcasted_iota(jnp.int32, (1, 128), 1) >> 5

    def one(step, chunk):
        tokens = []
        for i in range(CHUNK):
            item = work[step, chunk * CHUNK + i]
            if i == 0:
                block = item & 31
            tokens.append(own_ref[(item >> 5) & 1023])
            tokens.append(other_ref[item >> 15])
        inner = lax.dot_general(
            held_ref[block],
            jnp.concatenate(tokens, axis=0),
            (((1,), (1,)), ((), ())),
            preferred_element_type=jnp.float32,
        )
        kept = jnp.where(slots_id < lengths_ref[block], inner, -1e30)
        return jnp.max(kept, axis=0, keepdims=True)

    def steps(step, carry):
        done = [one(step, i) for i in range(TOGETHER)]
        for i, value in enumerate(done):
            for j in range(CHUNK):
                part = value[:, j // 4 * 128 : j // 4 * 128 + 128]
                dest = work[8 + step, i * CHUNK + j]
                best[pl.ds(dest, 1), :] = jnp.where(group == j % 4, part, 0.0)
        return carry

    lax.fori_loop(0, (total + TOGETHER - 1) // TOGETHER, steps, 0)
    lane = lax.broadcasted_iota(jnp.int32, (DEVICES, 128), 1)
    result = jnp.zeros((DEVICES, 128), jnp.float32)
    for rank in range(CAP):
        value = jnp.sum(best[pl.ds(rank * DEVICES, DEVICES), :], axis=1, keepdims=True)
        result = jnp.where(lane == rank, value * (1.0 / 32.0), result)
    out_ref[...] = result


def maxsim(where, lengths, own, other, held):
    return pl.pallas_call(
        maxsim_kernel,
        out_shape=jax.ShapeDtypeStruct((DEVICES, 128), jnp.float32),
        in_specs=[pl.BlockSpec(memory_space=SMEM)] * 2 + [pl.BlockSpec(memory_space=VMEM)] * 3,
        out_specs=pl.BlockSpec(memory_space=VMEM),
        scratch_shapes=[
            VMEM((DEVICES * 4, 128), jnp.float32),
            VMEM((16, 128), jnp.int32),
            SMEM((16, 128), jnp.int32),
            VMEM((DEVICES * CAP + 8, 128), jnp.float32),
            pltpu.SemaphoreType.DMA,
        ],
        compiler_params=pltpu.CompilerParams(vmem_limit_bytes=32 << 20),
        cost_estimate=pl.CostEstimate(flops=12000000, bytes_accessed=20000000, transcendentals=0),
        name="maxsim",
    )(where, lengths, own, other, held)


def pack_kernel(query_ref, ask_ref, out_ref):
    queries = query_ref.shape[0]
    out_ref[:queries] = query_ref[...]
    lane = lax.broadcasted_iota(jnp.int32, (1, 128), 1) >> 5
    wide = jnp.concatenate([ask_ref[...]] * 4, axis=1)
    rows = []
    for part in range(4):
        row = wide[4 * part : 4 * part + 1, :]
        for i in range(1, 4):
            row = jnp.where(lane == i, wide[4 * part + i : 4 * part + i + 1, :], row)
        rows.append(row)
    out_ref[queries] = jnp.concatenate(rows, axis=0).astype(jnp.bfloat16)


def pack(queries, asks):
    rows, tokens, width = queries.shape
    return pl.pallas_call(
        pack_kernel,
        out_shape=jax.ShapeDtypeStruct((rows + 1, tokens, width), jnp.bfloat16),
        in_specs=[pl.BlockSpec(memory_space=VMEM)] * 2,
        out_specs=pl.BlockSpec(memory_space=VMEM),
        compiler_params=pltpu.CompilerParams(vmem_limit_bytes=4 << 20),
        name="pack",
    )(queries, asks)


def final_kernel(owner_ref, back_ref, out_ref):
    per, queries = owner_ref.shape
    lane = lax.broadcasted_iota(jnp.int32, (128, queries), 0)
    named = [lane == owner_ref[c : c + 1, :] for c in range(per)]
    match = jnp.zeros((128, queries), jnp.float32)
    for mine in named:
        match += jnp.where(mine, 1.0, 0.0)
    row = lax.broadcasted_iota(jnp.int32, (queries, queries), 0)
    col = lax.broadcasted_iota(jnp.int32, (queries, queries), 1)
    prior = jnp.dot(
        match.astype(jnp.bfloat16), as_bf16(row < col), preferred_element_type=jnp.float32
    )
    back = back_ref[...]
    chosen = jnp.zeros((128, queries), jnp.float32)
    for rank in range(CAP):
        chosen = jnp.where(prior == float(rank), back[:, rank : rank + 1], chosen)
    for c in range(per):
        out_ref[c : c + 1, :] = jnp.sum(jnp.where(named[c], chosen, 0.0), axis=0, keepdims=True)


def final(owners, back):
    return pl.pallas_call(
        final_kernel,
        out_shape=jax.ShapeDtypeStruct(owners.shape, jnp.float32),
        in_specs=[pl.BlockSpec(memory_space=VMEM)] * 2,
        out_specs=pl.BlockSpec(memory_space=VMEM),
        compiler_params=pltpu.CompilerParams(vmem_limit_bytes=4 << 20),
        name="final",
    )(owners, back)


def relevance_of(tokens, centroids):
    token_count, query_rows, width = tokens.shape
    inner = lax.dot_general(
        tokens.reshape(token_count * query_rows, width),
        centroids,
        (((1,), (1,)), ((), ())),
        preferred_element_type=jnp.float32,
    )
    return jnp.max(inner.reshape(token_count, query_rows, -1), axis=0)


def per_device(queries, centroids, codes, scales, centroid_ids, lengths, owners, slots):
    query_rows = queries.shape[0]
    owner, slot = owners[0].T, slots[0].T
    asks = jnp.concatenate([owner, slot], axis=0).astype(jnp.float32)
    first = pack(queries, asks)
    by_x = jnp.stack([first if k == 0 else moved(first, along_x(k)) for k in X_STEPS], axis=1)
    by_x = by_x.reshape(query_rows + 1, SIDE * 4, 128)
    second = jnp.stack(
        [by_x if k == 0 else moved(by_x, along_first(k)) for k in FIRST_STEPS], axis=0
    )
    pieces = [second if k == 0 else moved(second, along_second(k)) for k in SECOND_STEPS]
    peers = [moved(piece, other_core) for piece in pieces]
    own = jnp.concatenate(pieces, axis=0).reshape(-1, SIDE * 4, 128)
    other = jnp.zeros((SIDE * SIDE, query_rows + 1, SIDE * 4, 128), queries.dtype)
    for i, piece in enumerate(peers):
        other = lax.dynamic_update_slice(other, piece, (i * SIDE, 0, 0, 0))
    other = other.reshape(-1, SIDE * 4, 128)

    lists, score = lax.axis_index("lists"), lax.axis_index("score")
    where = jnp.stack(
        [lists * 16 + score, lists // 2, lists % 2, score // SIDE, score % SIDE]
    ).astype(jnp.int32)
    held = rebuild(codes, scales, centroid_ids, centroids, second)
    totals = maxsim(where, lengths, own, other, held)
    outgoing = totals.reshape(DEVICES, 1, 128)
    back = lax.all_to_all(outgoing, AXES, split_axis=0, concat_axis=0, tiled=True)
    scores = final(owner, back.reshape(DEVICES, 128)).T
    tokens = jnp.concatenate([by_x[:query_rows], peers[0][0, :query_rows]], axis=1)
    relevance = relevance_of(jnp.swapaxes(tokens, 0, 1), centroids)
    return (scores[None], relevance)


def solution(mesh):
    placed = (
        P("score", "lists", None),
        P("lists", None),
        P(("lists", "score"), None, None),
        P(("lists", "score"), None),
        P(("lists", "score"), None),
        P(("lists", "score")),
        P("lists", "score", None),
        P("lists", "score", None),
    )
    return jax.shard_map(
        per_device,
        mesh=mesh,
        in_specs=placed,
        out_specs=(P("lists", "score", None), P("score", "lists")),
        check_vma=False,
    )
```

```python
import jax
import jax.numpy as jnp
from jax import lax
from jax.experimental import pallas as pl
from jax.experimental.pallas import tpu as pltpu
from jax.sharding import PartitionSpec as P

AXES = ("lists", "score")
SIDE = 4
CORES = 2
DEVICES = 128
CAP = 4
SMEM = pltpu.SMEM
VMEM = pltpu.VMEM


def device_of(x, core, y, z):
    x, y, z = x % SIDE, y % SIDE, z % SIDE
    return ((x * CORES + core) * SIDE + y) * SIDE + z


def moved(value, step):
    pairs = []
    for x in range(SIDE):
        for core in range(CORES):
            for y in range(SIDE):
                for z in range(SIDE):
                    pairs.append((device_of(x, core, y, z), device_of(*step(x, core, y, z))))
    return lax.ppermute(value, AXES, pairs)


def along_x(k):
    return lambda x, core, y, z: (x + k, core, y, z)


def along_first(k):
    return lambda x, core, y, z: (x, core, y + k, z) if core == 0 else (x, core, y, z + k)


def along_second(k):
    return lambda x, core, y, z: (x, core, y, z + k) if core == 0 else (x, core, y + k, z)


def other_core(x, core, y, z):
    return (x, 1 - core, y, z)


def rebuild_kernel(ids_ref, cent_ref, scale_ref, code_ref, _, out_ref, table, base):
    step = pl.program_id(0)

    @pl.when(step == 0)
    def _():
        table[...] = cent_ref[...].astype(jnp.float32)

    blocks, rows = code_ref.shape[:2]

    def one(b, carry):
        for p in range(rows):
            base[pl.ds(p, 1), :] = table[pl.ds(ids_ref[step * blocks + b, p], 1), :]
        scale = jnp.transpose(jnp.broadcast_to(scale_ref[b], (rows, rows)))
        value = base[...] + scale * code_ref[b].astype(jnp.float32)
        out_ref[b] = value.astype(jnp.bfloat16)
        return carry

    lax.fori_loop(0, blocks, one, 0)


def rebuild(codes, scales, centroid_ids, centroids, after):
    held, rows, width = codes.shape
    step = held // REBUILD_STEPS
    return pl.pallas_call(
        rebuild_kernel,
        grid=(REBUILD_STEPS,),
        out_shape=jax.ShapeDtypeStruct(codes.shape, jnp.bfloat16),
        in_specs=[
            pl.BlockSpec(memory_space=SMEM),
            pl.BlockSpec(centroids.shape, lambda b: (0, 0)),
            pl.BlockSpec((step, 1, rows), lambda b: (b, 0, 0)),
            pl.BlockSpec((step, rows, width), lambda b: (b, 0, 0)),
            pl.BlockSpec(memory_space=pl.ANY),
        ],
        out_specs=pl.BlockSpec((step, rows, width), lambda b: (b, 0, 0)),
        scratch_shapes=[
            VMEM(centroids.shape, jnp.float32),
            VMEM((rows, width), jnp.float32),
        ],
        compiler_params=pltpu.CompilerParams(vmem_limit_bytes=56 << 20),
        cost_estimate=pl.CostEstimate(flops=12000000, bytes_accessed=20000000, transcendentals=0),
        name="rebuild",
    )(centroid_ids, centroids, scales.reshape(held, 1, rows), codes, after)


REBUILD_STEPS = 4
CHUNK = 8
TOGETHER = 16
PLACES = 768
DUMMY_ROW = DEVICES * CAP
X_STEPS = (0, 1, 2, 3)
FIRST_STEPS = (0, 1, 2, 3)
SECOND_STEPS = (0, 1, 3, 2)


def as_bf16(mask):
    return jnp.where(mask, 1.0, 0.0).astype(jnp.bfloat16)


def product(a, b):
    return jnp.dot(a.astype(jnp.bfloat16), b, preferred_element_type=jnp.float32)


def picked(place, values):
    result = jnp.full(place.shape, values[-1], jnp.int32)
    for i, value in enumerate(values[:-1]):
        result = jnp.where(place == i, value, result)
    return result


def request_list(where_ref, own_ref, other_ref, meta):
    per = PER
    queries = per - 1
    me, my_x, my_core, my_y, my_z = (where_ref[i] for i in range(5))
    for half, ref in enumerate((own_ref, other_ref)):
        for i in range(SIDE * SIDE):
            meta[pl.ds((half * 16 + i) * 16, 16), :] = ref[i * per + queries].astype(jnp.float32)
    square = (DEVICES, 128)
    lane = lax.broadcasted_iota(jnp.int32, square, 1)
    line = lax.broadcasted_iota(jnp.int32, square, 0)
    lane_low, lane_high = lane & 31, lane >> 5
    line_low, line_high = line & 31, line >> 5
    same_low = as_bf16(line_low == lane_low)
    same_high = as_bf16(line_high == lane_high)
    parts = [meta[pl.ds(row, DEVICES, stride=4), :] for row in range(4)]
    mine = [parts[i] == me.astype(jnp.float32) for i in range(2)]
    hit = jnp.where(mine[0], 1.0, 0.0) + jnp.where(mine[1], 1.0, 0.0)
    slot = jnp.where(mine[0], parts[2], 0.0) + jnp.where(mine[1], parts[3], 0.0)
    earlier = as_bf16(line_low < lane_low)
    prior = product(hit, earlier)
    hit, slot = product(hit, same_low), product(slot, same_low)
    chosen = (hit > 0.5) & (prior == lane_high.astype(jnp.float32))
    low = lane_low.astype(jnp.float32)
    asked_query = product(jnp.where(chosen, low + 1.0, 0.0), same_high)
    asked_slot = product(jnp.where(chosen, slot, 0.0), same_high)
    wants = (asked_query > 0.5) & (asked_slot == low)
    before = product(jnp.where(lane < line, 1.0, 0.0), as_bf16(wants))
    count = jnp.sum(jnp.where(wants, 1.0, 0.0), axis=0, keepdims=True)
    count = jnp.broadcast_to(count, (8, 128))
    lower_ranks = product(count, as_bf16((line_low == lane_low) & (line_high < lane_high)))
    in_block = product(count, same_low)
    chunks = ((in_block.astype(jnp.int32) + (CHUNK - 1)) // CHUNK).astype(jnp.float32)
    first_chunk = product(chunks, as_bf16((line < 32) & (line < lane_low)))
    all_chunks = product(chunks, as_bf16(line < 32)).astype(jnp.int32)
    spot = before + lower_ranks[:1]
    spot_high = (spot.astype(jnp.int32) // CHUNK).astype(jnp.float32)
    spot_low = spot - spot_high * float(CHUNK)
    high = product(jnp.where(wants, spot_high + first_chunk[:1], 0.0), same_high)
    low_part = product(jnp.where(wants, spot_low, 0.0), same_high)
    spot = jnp.where(asked_query > 0.5, high * float(CHUNK) + low_part, -1.0).astype(jnp.int32)
    fields = [line.astype(jnp.float32), asked_query, asked_slot]
    u_row = lax.broadcasted_iota(jnp.int32, (8, 128), 1).astype(jnp.float32)
    kind = lax.broadcasted_iota(jnp.int32, (8, 128), 0)
    asked = [jnp.transpose(value) for value in fields[1:]]
    to = lax.broadcasted_iota(jnp.int32, (DEVICES, PLACES), 1)
    found = jnp.zeros((8, PLACES), jnp.float32)
    for rank in range(CAP):
        at = 32 * rank
        left = jnp.where(
            kind == 0,
            u_row,
            jnp.where(
                kind == 1,
                asked[0][at : at + 1, :],
                jnp.where(kind == 2, asked[1][at : at + 1, :], float(rank)),
            ),
        )
        found = found + product(left, as_bf16(spot[:, at : at + 1] == to))
    found = found.astype(jnp.int32)
    u, query, slot, rank = (found[i : i + 1, :] for i in range(4))
    half = u >> 6
    at = (u >> 2) & 15
    kx = picked(u & 3, X_STEPS)
    first, second = picked(at & 3, FIRST_STEPS), picked(at >> 2, SECOND_STEPS)
    turned_second = picked(at & 3, [SECOND_STEPS.index(step) for step in FIRST_STEPS])
    turned_first = picked(at >> 2, [FIRST_STEPS.index(step) for step in SECOND_STEPS])
    straight, turned = at, turned_second * 4 + turned_first
    own_at = jnp.where(half == 0, straight, turned) * per + query - 1
    other_at = jnp.where(half == 0, turned, straight) * per + query - 1
    core = my_core ^ half
    dy = jnp.where(core == 0, first, second)
    dz = jnp.where(core == 0, second, first)
    source = (((((my_x - kx) & 3) * 2 + core) * 4) + ((my_y - dy) & 3)) * 4 + ((my_z - dz) & 3)
    real = query > 0
    item = jnp.where(real, slot + (own_at << 5) + (other_at << 15), 0)
    goal = jnp.where(real, source + rank * DEVICES, DUMMY_ROW)
    return item, goal, all_chunks[:1]


PER = 33


def maxsim_kernel(
    where_ref, lengths_ref, own_ref, other_ref, held_ref, out_ref, meta, table, work, best, sem
):
    item, goal, all_chunks = request_list(where_ref, own_ref, other_ref, meta)
    for i in range(PLACES // 128):
        table[i : i + 1, :] = item[:, i * 128 : i * 128 + 128]
        table[8 + i : 9 + i, :] = goal[:, i * 128 : i * 128 + 128]
    table[7:8, :] = all_chunks
    copy = pltpu.make_async_copy(table, work, sem)
    copy.start()
    copy.wait()
    total = work[7, 0]
    slots_id = lax.broadcasted_iota(jnp.int32, (128, CHUNK * 32), 0)
    group = lax.broadcasted_iota(jnp.int32, (1, 128), 1) >> 5

    def one(step, chunk):
        tokens = []
        for i in range(CHUNK):
            item = work[step, chunk * CHUNK + i]
            if i == 0:
                block = item & 31
            tokens.append(own_ref[(item >> 5) & 1023])
            tokens.append(other_ref[item >> 15])
        inner = lax.dot_general(
            held_ref[block],
            jnp.concatenate(tokens, axis=0),
            (((1,), (1,)), ((), ())),
            preferred_element_type=jnp.float32,
        )
        kept = jnp.where(slots_id < lengths_ref[block], inner, -1e30)
        return jnp.max(kept, axis=0, keepdims=True)

    def steps(step, carry):
        done = [one(step, i) for i in range(TOGETHER)]
        for i, value in enumerate(done):
            for j in range(CHUNK):
                part = value[:, j // 4 * 128 : j // 4 * 128 + 128]
                dest = work[8 + step, i * CHUNK + j]
                best[pl.ds(dest, 1), :] = jnp.where(group == j % 4, part, 0.0)
        return carry

    lax.fori_loop(0, (total + TOGETHER - 1) // TOGETHER, steps, 0)
    lane = lax.broadcasted_iota(jnp.int32, (DEVICES, 128), 1)
    result = jnp.zeros((DEVICES, 128), jnp.float32)
    for rank in range(CAP):
        value = jnp.sum(best[pl.ds(rank * DEVICES, DEVICES), :], axis=1, keepdims=True)
        result = jnp.where(lane == rank, value * (1.0 / 32.0), result)
    out_ref[...] = result


def maxsim(where, lengths, own, other, held):
    return pl.pallas_call(
        maxsim_kernel,
        out_shape=jax.ShapeDtypeStruct((DEVICES, 128), jnp.float32),
        in_specs=[pl.BlockSpec(memory_space=SMEM)] * 2 + [pl.BlockSpec(memory_space=VMEM)] * 3,
        out_specs=pl.BlockSpec(memory_space=VMEM),
        scratch_shapes=[
            VMEM((DEVICES * 4, 128), jnp.float32),
            VMEM((16, 128), jnp.int32),
            SMEM((16, 128), jnp.int32),
            VMEM((DEVICES * CAP + 8, 128), jnp.float32),
            pltpu.SemaphoreType.DMA,
        ],
        compiler_params=pltpu.CompilerParams(vmem_limit_bytes=32 << 20),
        cost_estimate=pl.CostEstimate(flops=12000000, bytes_accessed=20000000, transcendentals=0),
        name="maxsim",
    )(where, lengths, own, other, held)


def pack_kernel(query_ref, ask_ref, out_ref):
    queries = query_ref.shape[0]
    out_ref[:queries] = query_ref[...]
    lane = lax.broadcasted_iota(jnp.int32, (1, 128), 1) >> 5
    wide = jnp.concatenate([ask_ref[...]] * 4, axis=1)
    rows = []
    for part in range(4):
        row = wide[4 * part : 4 * part + 1, :]
        for i in range(1, 4):
            row = jnp.where(lane == i, wide[4 * part + i : 4 * part + i + 1, :], row)
        rows.append(row)
    out_ref[queries] = jnp.concatenate(rows, axis=0).astype(jnp.bfloat16)


def pack(queries, asks):
    rows, tokens, width = queries.shape
    return pl.pallas_call(
        pack_kernel,
        out_shape=jax.ShapeDtypeStruct((rows + 1, tokens, width), jnp.bfloat16),
        in_specs=[pl.BlockSpec(memory_space=VMEM)] * 2,
        out_specs=pl.BlockSpec(memory_space=VMEM),
        compiler_params=pltpu.CompilerParams(vmem_limit_bytes=4 << 20),
        name="pack",
    )(queries, asks)


def final_kernel(owner_ref, back_ref, out_ref):
    per, queries = owner_ref.shape
    lane = lax.broadcasted_iota(jnp.int32, (128, queries), 0)
    named = [lane == owner_ref[c : c + 1, :] for c in range(per)]
    match = jnp.zeros((128, queries), jnp.float32)
    for mine in named:
        match += jnp.where(mine, 1.0, 0.0)
    row = lax.broadcasted_iota(jnp.int32, (queries, queries), 0)
    col = lax.broadcasted_iota(jnp.int32, (queries, queries), 1)
    prior = jnp.dot(
        match.astype(jnp.bfloat16), as_bf16(row < col), preferred_element_type=jnp.float32
    )
    back = back_ref[...]
    chosen = jnp.zeros((128, queries), jnp.float32)
    for rank in range(CAP):
        chosen = jnp.where(prior == float(rank), back[:, rank : rank + 1], chosen)
    for c in range(per):
        out_ref[c : c + 1, :] = jnp.sum(jnp.where(named[c], chosen, 0.0), axis=0, keepdims=True)


def final(owners, back):
    return pl.pallas_call(
        final_kernel,
        out_shape=jax.ShapeDtypeStruct(owners.shape, jnp.float32),
        in_specs=[pl.BlockSpec(memory_space=VMEM)] * 2,
        out_specs=pl.BlockSpec(memory_space=VMEM),
        compiler_params=pltpu.CompilerParams(vmem_limit_bytes=4 << 20),
        name="final",
    )(owners, back)


def relevance_of(tokens, centroids):
    token_count, query_rows, width = tokens.shape
    inner = lax.dot_general(
        tokens.reshape(token_count * query_rows, width),
        centroids,
        (((1,), (1,)), ((), ())),
        preferred_element_type=jnp.float32,
    )
    return jnp.max(inner.reshape(token_count, query_rows, -1), axis=0)


def per_device(queries, centroids, codes, scales, centroid_ids, lengths, owners, slots):
    query_rows = queries.shape[0]
    owner, slot = owners[0].T, slots[0].T
    asks = jnp.concatenate([owner, slot], axis=0).astype(jnp.float32)
    first = pack(queries, asks)
    by_x = jnp.stack([first if k == 0 else moved(first, along_x(k)) for k in X_STEPS], axis=1)
    by_x = by_x.reshape(query_rows + 1, SIDE * 4, 128)
    second = jnp.stack(
        [by_x if k == 0 else moved(by_x, along_first(k)) for k in FIRST_STEPS], axis=0
    )
    pieces = [second if k == 0 else moved(second, along_second(k)) for k in SECOND_STEPS]
    peers = [moved(piece, other_core) for piece in pieces]
    own = jnp.concatenate(pieces, axis=0).reshape(-1, SIDE * 4, 128)
    other = jnp.zeros((SIDE * SIDE, query_rows + 1, SIDE * 4, 128), queries.dtype)
    for i, piece in enumerate(peers):
        other = lax.dynamic_update_slice(other, piece, (i * SIDE, 0, 0, 0))
    other = other.reshape(-1, SIDE * 4, 128)

    lists, score = lax.axis_index("lists"), lax.axis_index("score")
    where = jnp.stack(
        [lists * 16 + score, lists // 2, lists % 2, score // SIDE, score % SIDE]
    ).astype(jnp.int32)
    held = rebuild(codes, scales, centroid_ids, centroids, second[1, 0])
    totals = maxsim(where, lengths, own, other, held)
    outgoing = totals.reshape(DEVICES, 1, 128)
    back = lax.all_to_all(outgoing, AXES, split_axis=0, concat_axis=0, tiled=True)
    scores = final(owner, back.reshape(DEVICES, 128)).T
    tokens = jnp.concatenate([by_x[:query_rows], peers[0][0, :query_rows]], axis=1)
    relevance = relevance_of(jnp.swapaxes(tokens, 0, 1), centroids)
    return (scores[None], relevance)


def solution(mesh):
    placed = (
        P("score", "lists", None),
        P("lists", None),
        P(("lists", "score"), None, None),
        P(("lists", "score"), None),
        P(("lists", "score"), None),
        P(("lists", "score")),
        P("lists", "score", None),
        P("lists", "score", None),
    )
    return jax.shard_map(
        per_device,
        mesh=mesh,
        in_specs=placed,
        out_specs=(P("lists", "score", None), P("score", "lists")),
        check_vma=False,
    )
```

```python
import jax
import jax.numpy as jnp
from jax import lax
from jax.experimental import pallas as pl
from jax.experimental.pallas import tpu as pltpu
from jax.sharding import PartitionSpec as P

AXES = ("lists", "score")
SIDE = 4
CORES = 2
DEVICES = 128
CAP = 4
SMEM = pltpu.SMEM
VMEM = pltpu.VMEM


def device_of(x, core, y, z):
    x, y, z = x % SIDE, y % SIDE, z % SIDE
    return ((x * CORES + core) * SIDE + y) * SIDE + z


def moved(value, step):
    pairs = []
    for x in range(SIDE):
        for core in range(CORES):
            for y in range(SIDE):
                for z in range(SIDE):
                    pairs.append((device_of(x, core, y, z), device_of(*step(x, core, y, z))))
    return lax.ppermute(value, AXES, pairs)


def along_x(k):
    return lambda x, core, y, z: (x + k, core, y, z)


def along_first(k):
    return lambda x, core, y, z: (x, core, y + k, z) if core == 0 else (x, core, y, z + k)


def along_second(k):
    return lambda x, core, y, z: (x, core, y, z + k) if core == 0 else (x, core, y + k, z)


def other_core(x, core, y, z):
    return (x, 1 - core, y, z)


def rebuild_kernel(ids_ref, cent_ref, scale_ref, code_ref, _, out_ref, table, base):
    step = pl.program_id(0)

    @pl.when(step == 0)
    def _():
        table[...] = cent_ref[...].astype(jnp.float32)

    blocks, rows = code_ref.shape[:2]

    def one(b, carry):
        for p in range(rows):
            base[pl.ds(p, 1), :] = table[pl.ds(ids_ref[step * blocks + b, p], 1), :]
        scale = jnp.transpose(jnp.broadcast_to(scale_ref[b], (rows, rows)))
        value = base[...] + scale * code_ref[b].astype(jnp.float32)
        out_ref[b] = value.astype(jnp.bfloat16)
        return carry

    lax.fori_loop(0, blocks, one, 0)


def rebuild(codes, scales, centroid_ids, centroids, after):
    held, rows, width = codes.shape
    step = held // REBUILD_STEPS
    return pl.pallas_call(
        rebuild_kernel,
        grid=(REBUILD_STEPS,),
        out_shape=jax.ShapeDtypeStruct(codes.shape, jnp.bfloat16),
        in_specs=[
            pl.BlockSpec(memory_space=SMEM),
            pl.BlockSpec(centroids.shape, lambda b: (0, 0)),
            pl.BlockSpec((step, 1, rows), lambda b: (b, 0, 0)),
            pl.BlockSpec((step, rows, width), lambda b: (b, 0, 0)),
            pl.BlockSpec(memory_space=pl.ANY),
        ],
        out_specs=pl.BlockSpec((step, rows, width), lambda b: (b, 0, 0)),
        scratch_shapes=[
            VMEM(centroids.shape, jnp.float32),
            VMEM((rows, width), jnp.float32),
        ],
        compiler_params=pltpu.CompilerParams(vmem_limit_bytes=56 << 20),
        cost_estimate=pl.CostEstimate(flops=12000000, bytes_accessed=20000000, transcendentals=0),
        name="rebuild",
    )(centroid_ids, centroids, scales.reshape(held, 1, rows), codes, after)


REBUILD_STEPS = 4
CHUNK = 8
TOGETHER = 16
PLACES = 768
DUMMY_ROW = DEVICES * CAP
X_STEPS = (0, 1, 2, 3)
FIRST_STEPS = (0, 1, 2, 3)
SECOND_STEPS = (0, 1, 3, 2)


def as_bf16(mask):
    return jnp.where(mask, 1.0, 0.0).astype(jnp.bfloat16)


def product(a, b):
    return jnp.dot(a.astype(jnp.bfloat16), b, preferred_element_type=jnp.float32)


def picked(place, values):
    result = jnp.full(place.shape, values[-1], jnp.int32)
    for i, value in enumerate(values[:-1]):
        result = jnp.where(place == i, value, result)
    return result


def request_list(where_ref, own_ref, other_ref, meta):
    per = PER
    queries = per - 1
    me, my_x, my_core, my_y, my_z = (where_ref[i] for i in range(5))
    for half, ref in enumerate((own_ref, other_ref)):
        for i in range(SIDE * SIDE):
            meta[pl.ds((half * 16 + i) * 16, 16), :] = ref[i * per + queries].astype(jnp.float32)
    square = (DEVICES, 128)
    lane = lax.broadcasted_iota(jnp.int32, square, 1)
    line = lax.broadcasted_iota(jnp.int32, square, 0)
    lane_low, lane_high = lane & 31, lane >> 5
    line_low, line_high = line & 31, line >> 5
    same_low = as_bf16(line_low == lane_low)
    same_high = as_bf16(line_high == lane_high)
    parts = [meta[pl.ds(row, DEVICES, stride=4), :] for row in range(4)]
    mine = [parts[i] == me.astype(jnp.float32) for i in range(2)]
    hit = jnp.where(mine[0], 1.0, 0.0) + jnp.where(mine[1], 1.0, 0.0)
    slot = jnp.where(mine[0], parts[2], 0.0) + jnp.where(mine[1], parts[3], 0.0)
    earlier = as_bf16(line_low < lane_low)
    prior = product(hit, earlier)
    hit, slot = product(hit, same_low), product(slot, same_low)
    chosen = (hit > 0.5) & (prior == lane_high.astype(jnp.float32))
    low = lane_low.astype(jnp.float32)
    asked_query = product(jnp.where(chosen, low + 1.0, 0.0), same_high)
    asked_slot = product(jnp.where(chosen, slot, 0.0), same_high)
    wants = (asked_query > 0.5) & (asked_slot == low)
    before = product(jnp.where(lane < line, 1.0, 0.0), as_bf16(wants))
    count = jnp.sum(jnp.where(wants, 1.0, 0.0), axis=0, keepdims=True)
    count = jnp.broadcast_to(count, (8, 128))
    lower_ranks = product(count, as_bf16((line_low == lane_low) & (line_high < lane_high)))
    in_block = product(count, same_low)
    chunks = ((in_block.astype(jnp.int32) + (CHUNK - 1)) // CHUNK).astype(jnp.float32)
    first_chunk = product(chunks, as_bf16((line < 32) & (line < lane_low)))
    all_chunks = product(chunks, as_bf16(line < 32)).astype(jnp.int32)
    spot = before + lower_ranks[:1]
    spot_high = (spot.astype(jnp.int32) // CHUNK).astype(jnp.float32)
    spot_low = spot - spot_high * float(CHUNK)
    high = product(jnp.where(wants, spot_high + first_chunk[:1], 0.0), same_high)
    low_part = product(jnp.where(wants, spot_low, 0.0), same_high)
    spot = jnp.where(asked_query > 0.5, high * float(CHUNK) + low_part, -1.0).astype(jnp.int32)
    fields = [line.astype(jnp.float32), asked_query, asked_slot]
    u_row = lax.broadcasted_iota(jnp.int32, (8, 128), 1).astype(jnp.float32)
    kind = lax.broadcasted_iota(jnp.int32, (8, 128), 0)
    asked = [jnp.transpose(value) for value in fields[1:]]
    to = lax.broadcasted_iota(jnp.int32, (DEVICES, PLACES), 1)
    found = jnp.zeros((8, PLACES), jnp.float32)
    for rank in range(CAP):
        at = 32 * rank
        left = jnp.where(
            kind == 0,
            u_row,
            jnp.where(
                kind == 1,
                asked[0][at : at + 1, :],
                jnp.where(kind == 2, asked[1][at : at + 1, :], float(rank)),
            ),
        )
        found = found + product(left, as_bf16(spot[:, at : at + 1] == to))
    found = found.astype(jnp.int32)
    u, query, slot, rank = (found[i : i + 1, :] for i in range(4))
    half = u >> 6
    at = (u >> 2) & 15
    kx = picked(u & 3, X_STEPS)
    first, second = picked(at & 3, FIRST_STEPS), picked(at >> 2, SECOND_STEPS)
    turned_second = picked(at & 3, [SECOND_STEPS.index(step) for step in FIRST_STEPS])
    turned_first = picked(at >> 2, [FIRST_STEPS.index(step) for step in SECOND_STEPS])
    straight, turned = at, turned_second * 4 + turned_first
    own_at = jnp.where(half == 0, straight, turned) * per + query - 1
    other_at = jnp.where(half == 0, turned, straight) * per + query - 1
    core = my_core ^ half
    dy = jnp.where(core == 0, first, second)
    dz = jnp.where(core == 0, second, first)
    source = (((((my_x - kx) & 3) * 2 + core) * 4) + ((my_y - dy) & 3)) * 4 + ((my_z - dz) & 3)
    real = query > 0
    item = jnp.where(real, slot + (own_at << 5) + (other_at << 15), 0)
    goal = jnp.where(real, source + rank * DEVICES, DUMMY_ROW)
    return item, goal, all_chunks[:1]


PER = 33


def maxsim_kernel(
    where_ref, own_ref, other_ref, held_ref, out_ref, meta, table, work, best, sem
):
    item, goal, all_chunks = request_list(where_ref, own_ref, other_ref, meta)
    for i in range(PLACES // 128):
        table[i : i + 1, :] = item[:, i * 128 : i * 128 + 128]
        table[8 + i : 9 + i, :] = goal[:, i * 128 : i * 128 + 128]
    table[7:8, :] = all_chunks
    copy = pltpu.make_async_copy(table, work, sem)
    copy.start()
    copy.wait()
    total = work[7, 0]
    slots_id = lax.broadcasted_iota(jnp.int32, (128, CHUNK * 32), 0)
    group = lax.broadcasted_iota(jnp.int32, (1, 128), 1) >> 5

    def one(step, chunk):
        tokens = []
        for i in range(CHUNK):
            item = work[step, chunk * CHUNK + i]
            if i == 0:
                block = item & 31
            tokens.append(own_ref[(item >> 5) & 1023])
            tokens.append(other_ref[item >> 15])
        inner = lax.dot_general(
            held_ref[block],
            jnp.concatenate(tokens, axis=0),
            (((1,), (1,)), ((), ())),
            preferred_element_type=jnp.float32,
        )
        kept = jnp.where(slots_id < where_ref[5 + block], inner, -1e30)
        return jnp.max(kept, axis=0, keepdims=True)

    def steps(step, carry):
        done = [one(step, i) for i in range(TOGETHER)]
        for i, value in enumerate(done):
            for j in range(CHUNK):
                part = value[:, j // 4 * 128 : j // 4 * 128 + 128]
                dest = work[8 + step, i * CHUNK + j]
                best[pl.ds(dest, 1), :] = jnp.where(group == j % 4, part, 0.0)
        return carry

    lax.fori_loop(0, (total + TOGETHER - 1) // TOGETHER, steps, 0)
    lane = lax.broadcasted_iota(jnp.int32, (DEVICES, 128), 1)
    result = jnp.zeros((DEVICES, 128), jnp.float32)
    for rank in range(CAP):
        value = jnp.sum(best[pl.ds(rank * DEVICES, DEVICES), :], axis=1, keepdims=True)
        result = jnp.where(lane == rank, value * (1.0 / 32.0), result)
    out_ref[...] = result


def maxsim(where, lengths, own, other, held):
    return pl.pallas_call(
        maxsim_kernel,
        out_shape=jax.ShapeDtypeStruct((DEVICES, 128), jnp.float32),
        in_specs=[pl.BlockSpec(memory_space=SMEM)] + [pl.BlockSpec(memory_space=VMEM)] * 3,
        out_specs=pl.BlockSpec(memory_space=VMEM),
        scratch_shapes=[
            VMEM((DEVICES * 4, 128), jnp.float32),
            VMEM((16, 128), jnp.int32),
            SMEM((16, 128), jnp.int32),
            VMEM((DEVICES * CAP + 8, 128), jnp.float32),
            pltpu.SemaphoreType.DMA,
        ],
        compiler_params=pltpu.CompilerParams(vmem_limit_bytes=32 << 20),
        cost_estimate=pl.CostEstimate(flops=12000000, bytes_accessed=20000000, transcendentals=0),
        name="maxsim",
    )(jnp.concatenate([where, lengths]), own, other, held)


def pack_kernel(query_ref, ask_ref, out_ref):
    queries = query_ref.shape[0]
    out_ref[:queries] = query_ref[...]
    lane = lax.broadcasted_iota(jnp.int32, (1, 128), 1) >> 5
    wide = jnp.concatenate([ask_ref[...]] * 4, axis=1)
    rows = []
    for part in range(4):
        row = wide[4 * part : 4 * part + 1, :]
        for i in range(1, 4):
            row = jnp.where(lane == i, wide[4 * part + i : 4 * part + i + 1, :], row)
        rows.append(row)
    out_ref[queries] = jnp.concatenate(rows, axis=0).astype(jnp.bfloat16)


def pack(queries, asks):
    rows, tokens, width = queries.shape
    return pl.pallas_call(
        pack_kernel,
        out_shape=jax.ShapeDtypeStruct((rows + 1, tokens, width), jnp.bfloat16),
        in_specs=[pl.BlockSpec(memory_space=VMEM)] * 2,
        out_specs=pl.BlockSpec(memory_space=VMEM),
        compiler_params=pltpu.CompilerParams(vmem_limit_bytes=4 << 20),
        name="pack",
    )(queries, asks)


def final_kernel(owner_ref, back_ref, out_ref):
    per, queries = owner_ref.shape
    lane = lax.broadcasted_iota(jnp.int32, (128, queries), 0)
    named = [lane == owner_ref[c : c + 1, :] for c in range(per)]
    match = jnp.zeros((128, queries), jnp.float32)
    for mine in named:
        match += jnp.where(mine, 1.0, 0.0)
    row = lax.broadcasted_iota(jnp.int32, (queries, queries), 0)
    col = lax.broadcasted_iota(jnp.int32, (queries, queries), 1)
    prior = jnp.dot(
        match.astype(jnp.bfloat16), as_bf16(row < col), preferred_element_type=jnp.float32
    )
    back = back_ref[...]
    chosen = jnp.zeros((128, queries), jnp.float32)
    for rank in range(CAP):
        chosen = jnp.where(prior == float(rank), back[:, rank : rank + 1], chosen)
    for c in range(per):
        out_ref[c : c + 1, :] = jnp.sum(jnp.where(named[c], chosen, 0.0), axis=0, keepdims=True)


def final(owners, back):
    return pl.pallas_call(
        final_kernel,
        out_shape=jax.ShapeDtypeStruct(owners.shape, jnp.float32),
        in_specs=[pl.BlockSpec(memory_space=VMEM)] * 2,
        out_specs=pl.BlockSpec(memory_space=VMEM),
        compiler_params=pltpu.CompilerParams(vmem_limit_bytes=4 << 20),
        name="final",
    )(owners, back)


def relevance_of(tokens, centroids):
    token_count, query_rows, width = tokens.shape
    inner = lax.dot_general(
        tokens.reshape(token_count * query_rows, width),
        centroids,
        (((1,), (1,)), ((), ())),
        preferred_element_type=jnp.float32,
    )
    return jnp.max(inner.reshape(token_count, query_rows, -1), axis=0)


def per_device(queries, centroids, codes, scales, centroid_ids, lengths, owners, slots):
    query_rows = queries.shape[0]
    owner, slot = owners[0].T, slots[0].T
    asks = jnp.concatenate([owner, slot], axis=0).astype(jnp.float32)
    first = pack(queries, asks)
    by_x = jnp.stack([first if k == 0 else moved(first, along_x(k)) for k in X_STEPS], axis=1)
    by_x = by_x.reshape(query_rows + 1, SIDE * 4, 128)
    second = jnp.stack(
        [by_x if k == 0 else moved(by_x, along_first(k)) for k in FIRST_STEPS], axis=0
    )
    pieces = [second if k == 0 else moved(second, along_second(k)) for k in SECOND_STEPS]
    peers = [moved(piece, other_core) for piece in pieces]
    own = jnp.concatenate(pieces, axis=0).reshape(-1, SIDE * 4, 128)
    other = jnp.zeros((SIDE * SIDE, query_rows + 1, SIDE * 4, 128), queries.dtype)
    for i, piece in enumerate(peers):
        other = lax.dynamic_update_slice(other, piece, (i * SIDE, 0, 0, 0))
    other = other.reshape(-1, SIDE * 4, 128)

    lists, score = lax.axis_index("lists"), lax.axis_index("score")
    where = jnp.stack(
        [lists * 16 + score, lists // 2, lists % 2, score // SIDE, score % SIDE]
    ).astype(jnp.int32)
    held = rebuild(codes, scales, centroid_ids, centroids, second[1, 0])
    totals = maxsim(where, lengths, own, other, held)
    outgoing = totals.reshape(DEVICES, 1, 128)
    back = lax.all_to_all(outgoing, AXES, split_axis=0, concat_axis=0, tiled=True)
    scores = final(owner, back.reshape(DEVICES, 128)).T
    tokens = jnp.concatenate([by_x[:query_rows], peers[0][0, :query_rows]], axis=1)
    relevance = relevance_of(jnp.swapaxes(tokens, 0, 1), centroids)
    return (scores[None], relevance)


def solution(mesh):
    placed = (
        P("score", "lists", None),
        P("lists", None),
        P(("lists", "score"), None, None),
        P(("lists", "score"), None),
        P(("lists", "score"), None),
        P(("lists", "score")),
        P("lists", "score", None),
        P("lists", "score", None),
    )
    return jax.shard_map(
        per_device,
        mesh=mesh,
        in_specs=placed,
        out_specs=(P("lists", "score", None), P("score", "lists")),
        check_vma=False,
    )
```
